32 devices in a mesh: freq: 4 (over z), space: 8 (over y, x, core).
Axes of the slice: x: 2, y: 2, z: 4, core: 2. Of those that a mesh axis runs over, the one named last changes fastest.
Arguments:
- direct: bfloat16 [2, 512, 65536], P(None, 'freq', 'space'), may hold values from -6 to 6
- adjoint: bfloat16 [2, 512, 65536], P(None, 'freq', 'space'), may hold values from -3.0517578e-05 to 3.0517578e-05
- coupling: float32 [7, 65536], P(None, 'space'), may hold values from 0.25 to 2
- wall: int32 [65536], P('space'), may hold values 0 or 1
Outputs:
- modes: bfloat16 [2, 512, 65536], P(None, 'freq', 'space')
- reduced: float32 [2, 512, 512], replicated
The draws below stay inside these ranges and needn't reach their ends.
All inputs are finite; a program needn't handle non-finite values. No bound on the sum of `wall` on one device may be relied on, other than what follows from the above.
Results may differ from the reference program's by a relative error of at most 0.007.
Values may be sent and summed in bfloat16 or wider, within the bound.
A program may use at most 128 MiB of HBM per device.

```python
import jax
import jax.numpy as jnp
from jax import lax

COLS = 512
NY = 64
NZ = 64
ITERS = 2
NCELL = 65536


def place_ends(entries, own_key, smallest, top_value):
    dims = entries.shape
    index_at = [jax.random.randint(jax.random.fold_in(own_key, axis), (), 0, dims[axis]) for axis in range(len(dims))]
    entries = entries.at[tuple(index_at)].set(smallest)
    longest = dims.index(max(dims))
    index_at[longest] = (index_at[longest] + 1) % dims[longest]
    return entries.at[tuple(index_at)].set(top_value)


def level_of(own_key, dims, pieces, smallest, largest):
    level = 1.0
    for axis_at, shards_of in pieces:
        draws = jax.random.uniform(jax.random.fold_in(jax.random.fold_in(own_key, 6), axis_at), (shards_of,), jnp.float32, smallest / len(pieces), largest / len(pieces))
        level = level * jnp.repeat(jnp.exp(draws), dims[axis_at] // shards_of).reshape((-1,) + (1,) * (len(dims) - 1 - axis_at))
    return level


def scatter_about(stream_key, dims, spread, limit, split=(), kind=jnp.bfloat16):
    entries = jax.random.normal(stream_key, dims, jnp.float32) * spread
    if len(split) > 0:
        entries = level_of(stream_key, dims, split, -0.22, 0.18) * entries
    return jnp.clip(entries, min=-limit, max=limit).astype(kind)


def setup_inputs(seed: int = 0) -> dict:
    splits = jax.random.split(jax.random.key(seed), 5)
    direct = scatter_about(splits[0], (2, COLS, NCELL), 1.0, 6.0, ((1, 4), (2, 8)))
    adjoint = scatter_about(splits[1], (2, COLS, NCELL), (2 * NCELL * COLS * COLS) ** -0.5, 3.0517578125e-05, ((1, 4), (2, 8)))
    coupling = jnp.clip(0.25 + 1.75 * jax.random.uniform(splits[2], (7, NCELL), jnp.float32) ** level_of(splits[2], (7, NCELL), ((1, 8),), -0.2, 0.2), 0.25, 2.0)
    wall = place_ends((jax.random.randint(splits[3], (NCELL,), 0, 8) < 1).astype(jnp.int32), jax.random.fold_in(splits[3], 1), 0, 1)
    return {"direct": direct, "adjoint": adjoint, "coupling": coupling, "wall": wall}


def complex_product(left_re, left_im, right_re, right_im):
    highest = lax.Precision.HIGHEST
    out_re = jnp.dot(left_re, right_re, precision=highest) - jnp.dot(left_im, right_im, precision=highest)
    out_im = jnp.dot(left_re, right_im, precision=highest) + jnp.dot(left_im, right_re, precision=highest)
    return out_re, out_im


def newton_schulz(hank_re, hank_im):
    total = jnp.sum(hank_re * hank_re + hank_im * hank_im)
    factor = 2.0 / total
    inverse_re = factor * hank_re.T
    inverse_im = -factor * hank_im.T
    identity = jnp.eye(hank_re.shape[0], dtype=jnp.float32)
    for iteration in range(ITERS):
        prod_re, prod_im = complex_product(hank_re, hank_im, inverse_re, inverse_im)
        inverse_re, inverse_im = complex_product(inverse_re, inverse_im, 2.0 * identity - prod_re, -prod_im)
    return inverse_re, inverse_im


def apply_operator(padded, coupling_local, wall_local, span_z):
    inner = padded[:, 1:-1]
    width = inner.shape[2]
    zero_rows = jnp.zeros(inner.shape[:2] + (span_z,), inner.dtype)
    zero_one = zero_rows[:, :, :1]
    north = jnp.concatenate([inner[:, :, span_z:], zero_rows], 2)
    south = jnp.concatenate([zero_rows, inner[:, :, :width - span_z]], 2)
    east = jnp.concatenate([inner[:, :, 1:], zero_one], 2)
    west = jnp.concatenate([zero_one, inner[:, :, :width - 1]], 2)
    zpos = jnp.arange(width, dtype=jnp.int32) % span_z
    east = jnp.where(zpos == span_z - 1, jnp.zeros_like(east), east)
    west = jnp.where(zpos == 0, jnp.zeros_like(west), west)
    beside = coupling_local[1] * padded[:, 2:] + coupling_local[2] * padded[:, :-2]
    beside = beside + coupling_local[3] * north + coupling_local[4] * south
    beside = beside + coupling_local[5] * east + coupling_local[6] * west
    result = coupling_local[0] * inner - beside
    return jnp.where(wall_local == 1, inner.astype(result.dtype), result)


def reference(direct, adjoint, coupling, wall):
    columns = direct.shape[1]
    ncells = direct.shape[2]
    plane = NY * NZ
    planes_all = ncells // plane
    adj_cat = jnp.concatenate([adjoint[0], adjoint[1]], 1)
    dir_stack = jnp.concatenate([jnp.concatenate([direct[0], direct[1]], 1), jnp.concatenate([direct[1], -direct[0]], 1)], 0)
    hank = lax.dot_general(adj_cat, dir_stack, (((1,), (1,)), ((), ())), preferred_element_type=jnp.float32)
    inverse_re, inverse_im = newton_schulz(hank[:, :columns], hank[:, columns:])
    bal_re = inverse_re.astype(jnp.bfloat16)
    bal_im = inverse_im.astype(jnp.bfloat16)
    mapping = jnp.concatenate([jnp.concatenate([bal_re.T, -bal_im.T], 1), jnp.concatenate([bal_im.T, bal_re.T], 1)], 0)
    phi = jnp.dot(mapping, jnp.concatenate([direct[0], direct[1]], 0), preferred_element_type=jnp.float32)
    modes = phi.astype(jnp.bfloat16).reshape(2, columns, ncells)
    field = phi.reshape(2 * columns, planes_all, plane)
    padded = jnp.pad(field, ((0, 0), (1, 1), (0, 0)))
    image = apply_operator(padded, coupling.reshape(7, planes_all, plane), wall.reshape(planes_all, plane), NZ)
    image = image.reshape(2, columns, ncells)
    img_stack = jnp.concatenate([jnp.concatenate([image[0], image[1]], 1), jnp.concatenate([image[1], -image[0]], 1)], 0)
    projected = lax.dot_general(adj_cat.astype(jnp.float32), img_stack, (((1,), (1,)), ((), ())), precision=lax.Precision.HIGHEST)
    scale_out = columns / 16.0
    reduced = scale_out * jnp.stack([projected[:, :columns], projected[:, columns:]], 0)
    return modes, reduced
```

```python
import jax
import jax.numpy as jnp
from jax import lax
from jax.experimental import pallas as pl
from jax.experimental.pallas import tpu as pltpu
from jax.sharding import PartitionSpec as P

NY = 64
NZ = 64
ITERS = 2


def complex_product(left_re, left_im, right_re, right_im):
    high = lax.Precision.HIGH
    out_re = jnp.dot(left_re, right_re, precision=high) - jnp.dot(
        left_im, right_im, precision=high
    )
    out_im = jnp.dot(left_re, right_im, precision=high) + jnp.dot(
        left_im, right_re, precision=high
    )
    return (out_re, out_im)


def newton_schulz(hank_re, hank_im):
    total = jnp.sum(hank_re * hank_re + hank_im * hank_im)
    factor = 2.0 / total
    inverse_re = factor * hank_re.T
    inverse_im = -factor * hank_im.T
    identity = jnp.eye(hank_re.shape[0], dtype=jnp.float32)
    for iteration in range(ITERS):
        prod_re, prod_im = complex_product(hank_re, hank_im, inverse_re, inverse_im)
        inverse_re, inverse_im = complex_product(
            inverse_re, inverse_im, 2.0 * identity - prod_re, -prod_im
        )
    return (inverse_re, inverse_im)


def stencil_kernel(planes, width, weights_ref, field_ref, banded_ref, low_ref, high_ref, out_ref):
    wide = width + 2 * NZ

    def plane_of(p):
        if p < 0:
            return low_ref[...]
        if p >= planes:
            return high_ref[...]
        return field_ref[:, p * width : (p + 1) * width]

    for p in range(planes):
        span = slice(p * width, (p + 1) * width)

        def weight(i):
            return weights_ref[i : i + 1, span]

        inner = plane_of(p).astype(jnp.float32)
        after = banded_ref[:, p * wide + 2 * NZ : (p + 1) * wide].astype(jnp.float32)
        before = banded_ref[:, p * wide : p * wide + width].astype(jnp.float32)
        beside = weight(1) * plane_of(p + 1).astype(jnp.float32)
        beside += weight(2) * plane_of(p - 1).astype(jnp.float32)
        beside += weight(3) * after
        beside += weight(4) * before
        beside += weight(5) * pltpu.roll(inner, width - 1, 1)
        beside += weight(6) * pltpu.roll(inner, 1, 1)
        out_ref[:, span] = (weight(0) * inner - beside).astype(out_ref.dtype)


def apply_operator(field, banded, low, high, weights, planes):
    rows, cells = field.shape
    width = cells // planes
    wide = width + 2 * NZ
    block = 64
    return pl.pallas_call(
        lambda *refs: stencil_kernel(planes, width, *refs),
        out_shape=jax.ShapeDtypeStruct((rows, cells), jnp.bfloat16),
        grid=(rows // block,),
        in_specs=[
            pl.BlockSpec((7, cells), lambda i: (0, 0)),
            pl.BlockSpec((block, cells), lambda i: (i, 0)),
            pl.BlockSpec((block, planes * wide), lambda i: (i, 0)),
            pl.BlockSpec((block, width), lambda i: (i, 0)),
            pl.BlockSpec((block, width), lambda i: (i, 0)),
        ],
        out_specs=pl.BlockSpec((block, cells), lambda i: (i, 0)),
        cost_estimate=pl.CostEstimate(
            flops=rows * cells * 40, bytes_accessed=rows * cells * 10, transcendentals=0
        ),
    )(weights, field, banded, low, high)


def conj_moment(left, right, parts):
    gram = lax.dot_general(
        left, right, (((1,), (1,)), ((), ())), preferred_element_type=jnp.float32
    )
    cols = gram.shape[0] // (2 * parts)
    gram = gram.reshape(parts, 2, cols, parts, 2, cols)
    out_re = gram[:, 0, :, :, 0, :] + gram[:, 1, :, :, 1, :]
    out_im = gram[:, 0, :, :, 1, :] - gram[:, 1, :, :, 0, :]
    return jnp.stack([out_re.reshape(parts * cols, -1), out_im.reshape(parts * cols, -1)], 0)


def mapping_of(bal_re, bal_im, parts):
    cols = bal_re.shape[0] // parts
    top_re = bal_re.T.reshape(parts, 1, cols, parts, 1, cols)
    top_im = bal_im.T.reshape(parts, 1, cols, parts, 1, cols)
    upper = jnp.concatenate([top_re, -top_im], 4)
    lower = jnp.concatenate([top_im, top_re], 4)
    return jnp.concatenate([upper, lower], 1).reshape(2 * parts * cols, 2 * parts * cols)


def shards(direct, adjoint, coupling, wall):
    parts = lax.axis_size("freq")
    slabs = lax.axis_size("space")
    mine = lax.axis_index("freq")
    local_cols = direct.shape[1]
    cells = direct.shape[2]
    plane = NY * NZ
    planes = cells // plane
    width = plane // parts
    columns = parts * local_cols

    def exchange(values):
        pieces = values.reshape(2 * local_cols, planes, parts, width).transpose(2, 0, 1, 3)
        pieces = pieces.reshape(parts, 2 * local_cols, planes * width)
        pieces = lax.all_to_all(pieces, "freq", split_axis=0, concat_axis=0, tiled=True)
        return pieces.reshape(2 * columns, planes * width)

    dir_ex = exchange(direct)
    adj_ex = exchange(adjoint)

    up = [(i, i + 1) for i in range(slabs - 1)]
    low = lax.ppermute(dir_ex[:, (planes - 1) * width :], "space", up)
    high = lax.ppermute(dir_ex[:, :width], "space", [(b, a) for a, b in up])
    over = [(i, i + 1) for i in range(parts - 1)]
    field = dir_ex.reshape(2 * columns, planes, width)
    first = field[:, :, :NZ].reshape(2 * columns, planes * NZ)
    last = field[:, :, width - NZ :].reshape(2 * columns, planes * NZ)
    before = lax.ppermute(last, "freq", over).reshape(2 * columns, planes, NZ)
    after = lax.ppermute(first, "freq", [(b, a) for a, b in over])
    after = after.reshape(2 * columns, planes, NZ)
    banded = jnp.concatenate([before, field, after], 2).reshape(2 * columns, -1)

    pick = coupling.reshape(7, planes, parts, width)
    pick = lax.dynamic_index_in_dim(pick, mine, 2, False).reshape(7, planes * width)
    held = wall.reshape(planes, parts, width)
    held = lax.dynamic_index_in_dim(held, mine, 1, False).reshape(1, planes * width) == 1
    zpos = jnp.arange(planes * width, dtype=jnp.int32)[None] % NZ
    slot = jnp.arange(7, dtype=jnp.int32)[:, None]
    off = held | ((slot == 5) & (zpos == NZ - 1)) | ((slot == 6) & (zpos == 0))
    weights = jnp.where(slot == 0, jnp.where(held, 1.0, pick), jnp.where(off, 0.0, pick))

    image = apply_operator(dir_ex, banded, low, high, weights, planes)

    hank = lax.psum(conj_moment(adj_ex, dir_ex, parts), ("freq", "space"))
    moment = conj_moment(adj_ex, image, parts)
    hank, moment = lax.optimization_barrier((hank, moment))
    moment = lax.psum(moment, ("freq", "space"))
    inverse_re, inverse_im = newton_schulz(hank[0], hank[1])
    bal_re = inverse_re.astype(jnp.bfloat16)
    bal_im = inverse_im.astype(jnp.bfloat16)
    mapping = mapping_of(bal_re, bal_im, parts)
    phi = jnp.dot(mapping, dir_ex, preferred_element_type=jnp.float32).astype(jnp.bfloat16)
    phi = phi.reshape(parts, 2 * local_cols, planes * width)
    modes = lax.all_to_all(phi, "freq", split_axis=0, concat_axis=0, tiled=True)
    modes = modes.reshape(parts, 2 * local_cols, planes, width).transpose(1, 2, 0, 3)
    modes = modes.reshape(2, local_cols, cells)
    red_re, red_im = complex_product(
        moment[0], moment[1], bal_re.astype(jnp.float32), bal_im.astype(jnp.float32)
    )
    reduced = (columns / 16.0) * jnp.stack([red_re, red_im], 0)
    return (modes, reduced)


def solution(mesh):
    return jax.shard_map(
        shards,
        mesh=mesh,
        in_specs=(P(None, "freq", "space"), P(None, "freq", "space"), P(None, "space"), P("space")),
        out_specs=(P(None, "freq", "space"), P()),
        check_vma=False,
    )
```

```python
import jax
import jax.numpy as jnp
from jax import lax
from jax.experimental import pallas as pl
from jax.experimental.pallas import tpu as pltpu
from jax.sharding import PartitionSpec as P

NY = 64
NZ = 64
ITERS = 2


def complex_product(left_re, left_im, right_re, right_im):
    high = lax.Precision.HIGH
    out_re = jnp.dot(left_re, right_re, precision=high) - jnp.dot(
        left_im, right_im, precision=high
    )
    out_im = jnp.dot(left_re, right_im, precision=high) + jnp.dot(
        left_im, right_re, precision=high
    )
    return (out_re, out_im)


def newton_schulz(hank_re, hank_im):
    total = jnp.sum(hank_re * hank_re + hank_im * hank_im)
    factor = 2.0 / total
    inverse_re = factor * hank_re.T
    inverse_im = -factor * hank_im.T
    identity = jnp.eye(hank_re.shape[0], dtype=jnp.float32)
    for iteration in range(ITERS):
        prod_re, prod_im = complex_product(hank_re, hank_im, inverse_re, inverse_im)
        inverse_re, inverse_im = complex_product(
            inverse_re, inverse_im, 2.0 * identity - prod_re, -prod_im
        )
    return (inverse_re, inverse_im)


def stencil_kernel(planes, width, weights_ref, field_ref, banded_ref, low_ref, high_ref, out_ref):
    wide = width + 2 * NZ

    def plane_of(p):
        if p < 0:
            return low_ref[...]
        if p >= planes:
            return high_ref[...]
        return field_ref[:, p * width : (p + 1) * width]

    for p in range(planes):
        span = slice(p * width, (p + 1) * width)

        def weight(i):
            return weights_ref[i : i + 1, span]

        inner = plane_of(p).astype(jnp.float32)
        after = banded_ref[:, p * wide + 2 * NZ : (p + 1) * wide].astype(jnp.float32)
        before = banded_ref[:, p * wide : p * wide + width].astype(jnp.float32)
        beside = weight(1) * plane_of(p + 1).astype(jnp.float32)
        beside += weight(2) * plane_of(p - 1).astype(jnp.float32)
        beside += weight(3) * after
        beside += weight(4) * before
        beside += weight(5) * pltpu.roll(inner, width - 1, 1)
        beside += weight(6) * pltpu.roll(inner, 1, 1)
        out_ref[:, span] = (weight(0) * inner - beside).astype(out_ref.dtype)


def apply_operator(field, banded, low, high, weights, planes):
    rows, cells = field.shape
    width = cells // planes
    wide = width + 2 * NZ
    block = 64
    return pl.pallas_call(
        lambda *refs: stencil_kernel(planes, width, *refs),
        out_shape=jax.ShapeDtypeStruct((rows, cells), jnp.bfloat16),
        grid=(rows // block,),
        in_specs=[
            pl.BlockSpec((7, cells), lambda i: (0, 0)),
            pl.BlockSpec((block, cells), lambda i: (i, 0)),
            pl.BlockSpec((block, planes * wide), lambda i: (i, 0)),
            pl.BlockSpec((block, width), lambda i: (i, 0)),
            pl.BlockSpec((block, width), lambda i: (i, 0)),
        ],
        out_specs=pl.BlockSpec((block, cells), lambda i: (i, 0)),
        cost_estimate=pl.CostEstimate(
            flops=rows * cells * 40, bytes_accessed=rows * cells * 10, transcendentals=0
        ),
    )(weights, field, banded, low, high)


def conj_moment(left, right, parts):
    gram = lax.dot_general(
        left, right, (((1,), (1,)), ((), ())), preferred_element_type=jnp.float32
    )
    cols = gram.shape[0] // (2 * parts)
    gram = gram.reshape(parts, 2, cols, parts, 2, cols)
    out_re = gram[:, 0, :, :, 0, :] + gram[:, 1, :, :, 1, :]
    out_im = gram[:, 0, :, :, 1, :] - gram[:, 1, :, :, 0, :]
    return jnp.stack([out_re.reshape(parts * cols, -1), out_im.reshape(parts * cols, -1)], 0)


def mapping_of(bal_re, bal_im, parts):
    cols = bal_re.shape[0] // parts
    top_re = bal_re.T.reshape(parts, 1, cols, parts, 1, cols)
    top_im = bal_im.T.reshape(parts, 1, cols, parts, 1, cols)
    upper = jnp.concatenate([top_re, -top_im], 4)
    lower = jnp.concatenate([top_im, top_re], 4)
    return jnp.concatenate([upper, lower], 1).reshape(2 * parts * cols, 2 * parts * cols)


def shards(direct, adjoint, coupling, wall):
    parts = lax.axis_size("freq")
    slabs = lax.axis_size("space")
    mine = lax.axis_index("freq")
    local_cols = direct.shape[1]
    cells = direct.shape[2]
    plane = NY * NZ
    planes = cells // plane
    width = plane // parts
    columns = parts * local_cols

    def of_planes(values, start, size, stride):
        return jnp.concatenate(
            [values[:, p * stride + start : p * stride + start + size] for p in range(planes)], 1
        )

    def exchange(values):
        values = values.reshape(2 * local_cols, cells)
        pieces = jnp.stack([of_planes(values, f * width, width, plane) for f in range(parts)], 0)
        pieces = lax.all_to_all(pieces, "freq", split_axis=0, concat_axis=0, tiled=True)
        return pieces.reshape(2 * columns, planes * width)

    dir_ex = exchange(direct)
    adj_ex = exchange(adjoint)

    up = [(i, i + 1) for i in range(slabs - 1)]
    low = lax.ppermute(dir_ex[:, (planes - 1) * width :], "space", up)
    high = lax.ppermute(dir_ex[:, :width], "space", [(b, a) for a, b in up])
    over = [(i, i + 1) for i in range(parts - 1)]
    first = of_planes(dir_ex, 0, NZ, width)
    last = of_planes(dir_ex, width - NZ, NZ, width)
    before = lax.ppermute(last, "freq", over)
    after = lax.ppermute(first, "freq", [(b, a) for a, b in over])
    bands = []
    for p in range(planes):
        bands.append(before[:, p * NZ : (p + 1) * NZ])
        bands.append(dir_ex[:, p * width : (p + 1) * width])
        bands.append(after[:, p * NZ : (p + 1) * NZ])
    banded = jnp.concatenate(bands, 1)

    pick = coupling.reshape(7, planes, parts, width)
    pick = lax.dynamic_index_in_dim(pick, mine, 2, False).reshape(7, planes * width)
    held = wall.reshape(planes, parts, width)
    held = lax.dynamic_index_in_dim(held, mine, 1, False).reshape(1, planes * width) == 1
    zpos = jnp.arange(planes * width, dtype=jnp.int32)[None] % NZ
    slot = jnp.arange(7, dtype=jnp.int32)[:, None]
    off = held | ((slot == 5) & (zpos == NZ - 1)) | ((slot == 6) & (zpos == 0))
    weights = jnp.where(slot == 0, jnp.where(held, 1.0, pick), jnp.where(off, 0.0, pick))

    image = apply_operator(dir_ex, banded, low, high, weights, planes)

    hank = lax.psum(conj_moment(adj_ex, dir_ex, parts), ("freq", "space"))
    moment = conj_moment(adj_ex, image, parts)
    hank, moment = lax.optimization_barrier((hank, moment))
    moment = lax.psum(moment, ("freq", "space"))
    inverse_re, inverse_im = newton_schulz(hank[0], hank[1])
    bal_re = inverse_re.astype(jnp.bfloat16)
    bal_im = inverse_im.astype(jnp.bfloat16)
    mapping = mapping_of(bal_re, bal_im, parts)
    phi = jnp.dot(mapping, dir_ex, preferred_element_type=jnp.float32).astype(jnp.bfloat16)
    phi = phi.reshape(parts, 2 * local_cols, planes * width)
    phi, moment = lax.optimization_barrier((phi, moment))
    modes = lax.all_to_all(phi, "freq", split_axis=0, concat_axis=0, tiled=True)
    modes = jnp.concatenate(
        [modes[f, :, p * width : (p + 1) * width] for p in range(planes) for f in range(parts)], 1
    )
    modes = modes.reshape(2, local_cols, cells)
    red_re, red_im = complex_product(
        moment[0], moment[1], bal_re.astype(jnp.float32), bal_im.astype(jnp.float32)
    )
    reduced = (columns / 16.0) * jnp.stack([red_re, red_im], 0)
    return (modes, reduced)


def solution(mesh):
    return jax.shard_map(
        shards,
        mesh=mesh,
        in_specs=(P(None, "freq", "space"), P(None, "freq", "space"), P(None, "space"), P("space")),
        out_specs=(P(None, "freq", "space"), P()),
        check_vma=False,
    )
```
